512 devices in a mesh: tok: 128 (over z_lo, x, y), mem: 4 (over z_hi, core).
Axes of the slice: x: 4, y: 4, z: 16 (z_hi: 2, z_lo: 8; z = z_hi * 8 + z_lo), core: 2. Of those that a mesh axis runs over, the one named last changes fastest.
Arguments:
- query_states: bfloat16 [4, 32768, 1024], P('mem', 'tok'), may hold values from -8 to 8
- key_states: bfloat16 [4, 32768, 1024], P('mem', 'tok'), may hold values from -8 to 8
- value_states: bfloat16 [4, 32768, 1024], P('mem', 'tok'), may hold values from -6 to 6
- observed: bfloat16 [32768, 1024], P('tok'), may hold values from -8 to 8
- closing_projector: bfloat16 [1024, 1024], P(('tok', 'mem')), may hold values from -0.1875 to 0.1875
Outputs:
- grad_query: bfloat16 [4, 32768, 1024], P('mem', 'tok')
- grad_key: bfloat16 [4, 32768, 1024], P('mem', 'tok')
- grad_value: bfloat16 [4, 32768, 1024], P('mem', 'tok')
The draws below stay inside these ranges and needn't reach their ends.
All inputs are finite; a program needn't handle non-finite values.
Results may differ from the reference program's by a relative error of at most 0.035.
Values may be sent and summed in bfloat16 or wider, within the bound.
A program may use at most 128 MiB of HBM per device.

```python
import math
import jax
import jax.numpy as jnp
from jax import lax

LATENT_BREADTH = 1024
HEADS = 16
HD = 64
CELLS_IN_SLICE = 256
REACH = 128
COHORT_COUNT = 4
TOKENS = 32768


def draw_query_states(key, part):
    key = jax.random.fold_in(key, 1)
    full_shape = (COHORT_COUNT, TOKENS, LATENT_BREADTH)
    values = jnp.clip(jax.random.normal(key, full_shape), -6.0, 6.0)
    return values.astype(jnp.bfloat16)


def draw_key_states(key, part):
    key = jax.random.fold_in(key, 2)
    full_shape = (COHORT_COUNT, TOKENS, LATENT_BREADTH)
    values = jnp.clip(jax.random.normal(key, full_shape), -6.0, 6.0)
    return values.astype(jnp.bfloat16)


def draw_observed(key, part):
    key = jax.random.fold_in(key, 3)
    key_sign, key_size, key_noise = jax.random.split(key, 3)
    signs = jnp.where(jax.random.bernoulli(key_sign, 0.5, (1, LATENT_BREADTH)), 1.0, -1.0)
    sizes = jax.random.uniform(key_size, (1, LATENT_BREADTH), minval=1.5, maxval=3.5)
    full_shape = (TOKENS, LATENT_BREADTH)
    noise = jnp.clip(jax.random.normal(key_noise, full_shape), -3.5, 3.5)
    values = jnp.clip(signs * sizes + noise, -8.0, 8.0)
    return values.astype(jnp.bfloat16)


def levels(key, shape, cuts, smallest, top_value):
    factor_of, own = 1.0, jax.random.fold_in(key, 6)
    for dim, parts in cuts:
        steps = jnp.exp(jax.random.uniform(jax.random.fold_in(own, dim), (parts,), jnp.float32, smallest / len(cuts), top_value / len(cuts)))
        factor_of = factor_of * jnp.repeat(steps, shape[dim] // parts).reshape([-1 if axis == dim else 1 for axis in range(len(shape))])
    return factor_of


def centred(key, dims, deviation, limit, cuts=(), held_as=jnp.bfloat16):
    result = deviation * jax.random.normal(key, dims, jnp.float32)
    if cuts:
        result = result * levels(key, dims, cuts, -0.22, 0.18)
    return jnp.clip(result, -limit, limit).astype(held_as)


def setup_inputs(seed: int = 0) -> dict:
    splits = jax.random.split(jax.random.key(seed), 6)
    query_states = draw_query_states(jax.random.fold_in(splits[5], 71), 0)
    key_states = draw_key_states(jax.random.fold_in(splits[5], 71), 0)
    value_states = centred(splits[2], (COHORT_COUNT, TOKENS, LATENT_BREADTH), 1.0, 6.0, ((0, 4), (1, 128)))
    observed = draw_observed(jax.random.fold_in(splits[5], 71), 0)
    closing_projector = centred(splits[4], (LATENT_BREADTH, LATENT_BREADTH), LATENT_BREADTH ** -0.5, 0.1875, ((0, 512),))
    return dict(query_states=query_states, key_states=key_states, value_states=value_states, observed=observed, closing_projector=closing_projector)


def score_derivative(difference):
    return difference / jnp.sqrt(difference * difference + 0.25)

def reference(query_states, key_states, value_states, observed, closing_projector):
    block_count = TOKENS // CELLS_IN_SLICE
    key_span = CELLS_IN_SLICE + 2 * REACH
    score_scale = 1.0 / math.sqrt(HD)
    pad_spec = ((0, 0), (REACH, REACH), (0, 0))
    key_padded = jnp.pad(key_states, pad_spec)
    value_padded = jnp.pad(value_states, pad_spec)
    relative = jnp.arange(key_span, dtype=jnp.int32)[None, :] - REACH - jnp.arange(CELLS_IN_SLICE, dtype=jnp.int32)[:, None]
    band = jnp.abs(relative) <= REACH

    def step_block(accums, block_id):
        key_accum, value_accum = accums
        begin_row = (block_id * CELLS_IN_SLICE).astype(jnp.int32)
        anchor = jnp.zeros((), jnp.int32)
        queries = lax.dynamic_slice(query_states, (anchor, begin_row, anchor), (COHORT_COUNT, CELLS_IN_SLICE, LATENT_BREADTH))
        key_win = lax.dynamic_slice(key_padded, (anchor, begin_row, anchor), (COHORT_COUNT, key_span, LATENT_BREADTH))
        value_win = lax.dynamic_slice(value_padded, (anchor, begin_row, anchor), (COHORT_COUNT, key_span, LATENT_BREADTH))
        truth_analysis = lax.dynamic_slice(observed, (begin_row, anchor), (CELLS_IN_SLICE, LATENT_BREADTH)).astype(jnp.float32)
        position = begin_row + jnp.arange(key_span, dtype=jnp.int32) - REACH
        inside = (position >= 0) & (position < TOKENS)
        window_weight = jnp.where(band & inside[None, :], 1.0, 0.0).astype(jnp.float32)
        query_heads = queries.reshape(COHORT_COUNT, CELLS_IN_SLICE, HEADS, HD).astype(jnp.float32)
        key_heads = key_win.reshape(COHORT_COUNT, key_span, HEADS, HD).astype(jnp.float32)
        value_heads = value_win.reshape(COHORT_COUNT, key_span, HEADS, HD).astype(jnp.float32)
        scores = jnp.einsum('mihd,mjhd->mhij', query_heads, key_heads) * score_scale
        masked = jnp.where(window_weight[None, None] > 0, scores, -jnp.inf)
        row_max = lax.optimization_barrier(jnp.max(masked, axis=-1, keepdims=True))
        scaled = window_weight[None, None] * jnp.exp(masked - row_max)
        attn_prob = scaled / lax.optimization_barrier(jnp.sum(scaled, axis=-1, keepdims=True))
        prob_low = attn_prob.astype(jnp.bfloat16)
        mixed_context = jnp.einsum('mhij,mjhd->mihd', prob_low.astype(jnp.float32), value_heads)
        mixed_context = mixed_context.reshape(COHORT_COUNT * CELLS_IN_SLICE, LATENT_BREADTH).astype(jnp.bfloat16)
        predicted_latent = jnp.dot(mixed_context, closing_projector, preferred_element_type=jnp.float32).astype(jnp.bfloat16)
        predicted_maps = predicted_latent.reshape(COHORT_COUNT, CELLS_IN_SLICE, LATENT_BREADTH).astype(jnp.float32)
        couple_contributions = lax.optimization_barrier(jnp.sum(score_derivative(predicted_maps[:, None] - predicted_maps[None, :]), axis=1))
        prediction_adjoint = (score_derivative(predicted_maps - truth_analysis[None]) - couple_contributions / (COHORT_COUNT - 1)).astype(jnp.bfloat16)
        attended_grad = jnp.dot(prediction_adjoint.reshape(COHORT_COUNT * CELLS_IN_SLICE, LATENT_BREADTH), closing_projector.T, preferred_element_type=jnp.float32).astype(jnp.bfloat16)
        grad_heads = attended_grad.reshape(COHORT_COUNT, CELLS_IN_SLICE, HEADS, HD).astype(jnp.float32)
        prob_grad = jnp.einsum('mihd,mjhd->mhij', grad_heads, value_heads)
        row_dot = lax.optimization_barrier(jnp.sum(attn_prob * prob_grad, axis=-1, keepdims=True))
        score_grad = (attn_prob * (prob_grad - row_dot) * score_scale).astype(jnp.bfloat16)
        query_grad = jnp.einsum('mhij,mjhd->mihd', score_grad.astype(jnp.float32), key_heads)
        query_grad = query_grad.reshape(COHORT_COUNT, CELLS_IN_SLICE, LATENT_BREADTH).astype(jnp.bfloat16)
        key_terms = jnp.einsum('mhij,mihd->mjhd', score_grad.astype(jnp.float32), query_heads)
        value_terms = jnp.einsum('mhij,mihd->mjhd', prob_low.astype(jnp.float32), grad_heads)
        key_terms = key_terms.reshape(COHORT_COUNT, key_span, LATENT_BREADTH)
        value_terms = value_terms.reshape(COHORT_COUNT, key_span, LATENT_BREADTH)
        old_key = lax.dynamic_slice(key_accum, (anchor, begin_row, anchor), (COHORT_COUNT, key_span, LATENT_BREADTH))
        old_value = lax.dynamic_slice(value_accum, (anchor, begin_row, anchor), (COHORT_COUNT, key_span, LATENT_BREADTH))
        key_accum = lax.dynamic_update_slice(key_accum, old_key + key_terms, (anchor, begin_row, anchor))
        value_accum = lax.dynamic_update_slice(value_accum, old_value + value_terms, (anchor, begin_row, anchor))
        return ((key_accum, value_accum), query_grad)
    empty = jnp.zeros((COHORT_COUNT, TOKENS + 2 * REACH, LATENT_BREADTH), jnp.float32)
    block_ids = jnp.arange(block_count, dtype=jnp.int32)
    (key_accum, value_accum), query_blocks = lax.scan(step_block, (empty, empty), block_ids)
    grad_query = jnp.transpose(query_blocks, (1, 0, 2, 3)).reshape(COHORT_COUNT, TOKENS, LATENT_BREADTH)
    grad_key = key_accum[:, REACH:REACH + TOKENS].astype(jnp.bfloat16)
    grad_value = value_accum[:, REACH:REACH + TOKENS].astype(jnp.bfloat16)
    return (grad_query, grad_key, grad_value)
```

```python
import jax
import jax.numpy as jnp
from jax import lax
from jax.experimental import pallas as pl
from jax.experimental.pallas import tpu as pltpu
from jax.sharding import PartitionSpec as P

MESH = pl.DeviceIdType.MESH
F32 = jnp.float32
BF16 = jnp.bfloat16

TOK = 128
ROWS = 256
REACH = 128
WIDTH = 1024
HD = 64
TILE = 64
TILES = 4
WIN = TILE + 2 * REACH
LANES = 256
QUADS = 4
EXT = ROWS + 2 * REACH
BLOCKED = -1e30


def chip(x, y, z, c):
    return ((z % 8) * 16 + x * 4 + y, (z // 8) * 2 + c)


def dot(a, b, ca, cb):
    return lax.dot_general(a, b, (((ca,), (cb,)), ((), ())), preferred_element_type=F32)


def slope(d):
    return d * lax.rsqrt(d * d + 0.25)


def lanes_of(quad):
    return pl.ds(pl.multiple_of(quad * LANES, LANES), LANES)


def kernel(
    q_hbm, k_hbm, v_hbm, o_hbm, w_in,
    gq_hbm, gk_hbm, gv_hbm,
    q_s, kx, vx, obs, w_tmp, wg, wf, w_s, att, probs, rl_rows, rl_lanes, bias,
    dout, acc_k, acc_v, sbuf, rbuf, gq_s, gk_s, gv_s,
    load_sem, halo_ss, halo_rs, wz_ss, wz_rs, wn_ss, wn_rs, wy_ss, wy_rs, wx_ss, wx_rs, wc_ss, wc_rs,
    far_ss, far_rs, sib_ss, sib_rs, fwd_ss, fwd_rs, ret_ss, ret_rs, out_sem,
):
    tok = lax.axis_index("tok")
    mem = lax.axis_index("mem")
    x = (tok // 4) % 4
    y = tok % 4
    z = (mem // 2) * 8 + tok // 16
    c = mem % 2
    sibling = (tok, (mem // 2) * 2 + (1 - c))
    far = (tok, (mem + 2) % 4)
    lower = (tok - 1, mem)
    upper = (tok + 1, mem)
    has_lower = tok > 0
    has_upper = tok < TOK - 1

    def remote(src, dst, ss, rs, device):
        return pltpu.make_async_remote_copy(
            src_ref=src, dst_ref=dst, send_sem=ss, recv_sem=rs, device_id=device, device_id_type=MESH
        )

    barrier = pltpu.get_barrier_semaphore()

    def greet(device):
        pl.semaphore_signal(barrier, inc=1, device_id=device, device_id_type=MESH)

    greet(sibling)
    for d in (1, 2, 3):
        greet(chip(x, y, (z + 4 * d) % 16, c))
        greet(chip(x, y, (z + 16 - d) % 16, c))
        greet(chip(x, (y + d) % 4, z, c))
        greet(chip((x + d) % 4, y, z, c))

    @pl.when(has_lower)
    def _():
        greet(lower)

    @pl.when(has_upper)
    def _():
        greet(upper)

    own = pl.ds(REACH, ROWS)
    loads = [
        pltpu.make_async_copy(k_hbm.at[0], kx.at[own], load_sem.at[0]),
        pltpu.make_async_copy(q_hbm.at[0], q_s, load_sem.at[1]),
        pltpu.make_async_copy(v_hbm.at[0], vx.at[own], load_sem.at[2]),
        pltpu.make_async_copy(o_hbm, obs, load_sem.at[3]),
    ]
    for cp in loads:
        cp.start()

    mine = w_in[...].astype(F32)
    for r in range(2):
        for b in range(8):
            w_tmp[r * 8 + b : r * 8 + b + 1, :] = mine[r : r + 1, b * 128 : (b + 1) * 128]
    unit = ((c * 4 + x) * 4 + y) * 16 + (z % 4) * 4 + z // 4
    wg[unit] = w_tmp[...].astype(BF16)

    pl.semaphore_wait(
        barrier, 13 + jnp.where(has_lower, 1, 0) + jnp.where(has_upper, 1, 0)
    )

    def halo(side, kv, quad):
        src = (k_hbm, v_hbm)[kv]
        dst = (kx, vx)[kv]
        cols = lanes_of(quad)
        if side == 0:
            return remote(
                src.at[0, pl.ds(ROWS - REACH, REACH), cols], dst.at[pl.ds(0, REACH), cols],
                halo_ss.at[0, kv, quad], halo_rs.at[0, kv, quad], upper,
            )
        return remote(
            src.at[0, pl.ds(0, REACH), cols], dst.at[pl.ds(REACH + ROWS, REACH), cols],
            halo_ss.at[1, kv, quad], halo_rs.at[1, kv, quad], lower,
        )

    def start_halo(quad, carry):
        @pl.when(has_upper)
        def _():
            halo(0, 0, quad).start()
            halo(0, 1, quad).start()

        @pl.when(has_lower)
        def _():
            halo(1, 0, quad).start()
            halo(1, 1, quad).start()

        return carry

    lax.fori_loop(0, QUADS, start_halo, 0)

    def w_copy(first, count, ss, rs, device):
        block = wg.at[pl.ds(first, count)]
        return remote(block, block, ss, rs, device)

    def w_step(step, d, incoming):
        away = (z + 16 - 4 * d) % 16 if step == 0 else (z + 16 - d) % 16
        away = away if incoming else z
        plane = ((c * 4 + x) * 4 + y) * 16
        if step == 0:
            return w_copy(
                plane + (away % 4) * 4 + away // 4, 1, wz_ss.at[d - 1], wz_rs.at[d - 1],
                chip(x, y, (z + 4 * d) % 16, c),
            )
        if step == 1:
            return w_copy(
                plane + (away % 4) * 4, 4, wn_ss.at[d - 1], wn_rs.at[d - 1], chip(x, y, (z + d) % 16, c)
            )
        if step == 2:
            column = (y + 4 - d) % 4 if incoming else y
            return w_copy(
                ((c * 4 + x) * 4 + column) * 16, 16, wy_ss.at[d - 1], wy_rs.at[d - 1],
                chip(x, (y + d) % 4, z, c),
            )
        column = (x + 4 - d) % 4 if incoming else x
        return w_copy(
            (c * 4 + column) * 64, 64, wx_ss.at[d - 1], wx_rs.at[d - 1], chip((x + d) % 4, y, z, c)
        )

    def w_start(step):
        for d in (1, 2, 3):
            w_step(step, d, False).start()

    def w_wait(step):
        for d in (1, 2, 3):
            w_step(step, d, True).wait_recv()

    def w_sent(step):
        for d in (1, 2, 3):
            w_step(step, d, False).wait_send()

    w_sib_out = w_copy(c * 256, 256, wc_ss, wc_rs, sibling)
    w_sib_in = w_copy((1 - c) * 256, 256, wc_ss, wc_rs, sibling)

    w_start(0)

    row = lax.broadcasted_iota(jnp.int32, (WIN, LANES), 0)
    query = lax.broadcasted_iota(jnp.int32, (WIN, LANES), 1) % TILE
    band = (row >= query) & (row <= query + 2 * REACH)
    for t in range(TILES):
        place = row + TILE * t
        lowest = jnp.where(has_lower, 0, REACH)
        highest = jnp.where(has_upper, EXT, REACH + ROWS)
        inside = (place >= lowest) & (place < highest)
        bias[t] = jnp.where(band & inside, 0.0, BLOCKED)

    def zero(i, carry):
        rows = pl.ds(pl.multiple_of(i * 32, 32), 32)
        acc_k[rows, :] = jnp.zeros((32, WIDTH), F32)
        acc_v[rows, :] = jnp.zeros((32, WIDTH), F32)
        return carry

    lax.fori_loop(0, EXT // 32, zero, 0)

    @pl.when(jnp.logical_not(has_lower))
    def _():
        kx[pl.ds(0, REACH), :] = jnp.zeros((REACH, WIDTH), BF16)
        vx[pl.ds(0, REACH), :] = jnp.zeros((REACH, WIDTH), BF16)
        for slot in (1, 3):
            rbuf[slot] = jnp.zeros((2, TILE, WIDTH), BF16)

    @pl.when(jnp.logical_not(has_upper))
    def _():
        kx[pl.ds(REACH + ROWS, REACH), :] = jnp.zeros((REACH, WIDTH), BF16)
        vx[pl.ds(REACH + ROWS, REACH), :] = jnp.zeros((REACH, WIDTH), BF16)
        for slot in (0, 2):
            rbuf[slot] = jnp.zeros((2, TILE, WIDTH), BF16)

    for cp in loads:
        cp.wait()

    left_half = lax.broadcasted_iota(jnp.int32, (TILE, 128), 1) < HD

    def spread(pairs):
        none = jnp.zeros((TILE, 128), F32)
        rows = []
        for h in range(4):
            keep = left_half if h % 2 == 0 else jnp.logical_not(left_half)
            part = jnp.where(keep, pairs[h], 0.0)
            rows.append(jnp.concatenate([part, none] if h < 2 else [none, part], axis=1))
        return jnp.concatenate(rows, axis=0).astype(BF16)

    def tile_of(i):
        return i // 2 + (i % 2) * (3 - 2 * (i // 2))

    def query_block(t, quad):
        rows = pl.ds(pl.multiple_of(t * TILE, TILE), TILE)
        part = q_s[rows, lanes_of(quad)].astype(F32) * 0.125
        return spread([part[:, :128], part[:, :128], part[:, 128:], part[:, 128:]])

    def far_copy(i, quad):
        cols = lanes_of(quad)
        return remote(att.at[0, i, :, cols], att.at[2, i, :, cols], far_ss.at[i, quad], far_rs.at[i, quad], far)

    def fwd_copy(i, quad):
        cols = lanes_of(quad)
        return remote(att.at[2, i, :, cols], att.at[3, i, :, cols], fwd_ss.at[i, quad], fwd_rs.at[i, quad], sibling)

    def sib_copy(i):
        return remote(att.at[0, i], att.at[1, i], sib_ss.at[i], sib_rs.at[i], sibling)

    ones = jnp.ones((WIN, 128), BF16)

    def forward_quad(i, quad):
        t = tile_of(i)

        @pl.when((i == 0) & has_lower)
        def _():
            halo(0, 0, quad).wait_recv()
            halo(0, 1, quad).wait_recv()

        @pl.when((i == 1) & has_upper)
        def _():
            halo(1, 0, quad).wait_recv()
            halo(1, 1, quad).wait_recv()

        cols = lanes_of(quad)
        window = pl.ds(pl.multiple_of(t * TILE, TILE), WIN)
        scores = dot(kx[window, cols], query_block(t, quad), 1, 1) + bias[t]
        top = jnp.max(scores, axis=0, keepdims=True)
        weights = jnp.exp(scores - top).astype(BF16)
        total = jnp.sum(weights.astype(F32), axis=0, keepdims=True)
        n = i * QUADS + quad
        probs[n] = weights
        rl_lanes[n] = jnp.broadcast_to(1.0 / total, (8, LANES))
        values = vx[window, cols]
        halves = []
        for half in range(2):
            part = slice(half * 128, half * 128 + 128)
            rhs = jnp.concatenate([values[:, part], ones], axis=1)
            mixed = dot(weights[:, part], rhs, 0, 0)
            inverse = 1.0 / mixed[:, 128:]
            rl_rows[n, pl.ds(half * 128, 128), :] = inverse
            mixed = mixed[:, :128] * inverse
            halves.append(jnp.where(left_half, mixed[:TILE], mixed[TILE:]))
        att[0, i, :, cols] = jnp.concatenate(halves, axis=1).astype(BF16)
        far_copy(i, quad).start()

    def forward_tile(i, carry):
        def step(quad, inner):
            forward_quad(i, quad)
            return inner

        lax.fori_loop(0, QUADS, step, 0)
        sib_copy(i).start()

        @pl.when(i == 0)
        def _():
            w_wait(0)
            w_start(1)

        @pl.when(i == 1)
        def _():
            w_wait(1)
            w_start(2)

        @pl.when(i == 2)
        def _():
            w_wait(2)
            w_start(3)

        return carry

    lax.fori_loop(0, TILES, forward_tile, 0)

    w_wait(3)
    w_sib_out.start()
    w_sib_in.wait_recv()

    def place_units(n, carry):
        for zr in range(4):
            for zq in range(4):
                d = ((zq % 2) * 4 + zr) * 64 + (n % 16) * 4 + (zq // 2) * 2 + n // 16
                wf[pl.ds(pl.multiple_of(d * 16, 16), 16), :] = wg[n * 16 + zr * 4 + zq].astype(F32)
        return carry

    lax.fori_loop(0, 32, place_units, 0)

    def place_rows(n, carry):
        rows = pl.ds(pl.multiple_of(n * 128, 128), 128)
        for b in range(8):
            part = wf[pl.ds(n * 1024 + b, 128, stride=8), :]
            w_s[rows, b * 128 : (b + 1) * 128] = part.astype(BF16)
        return carry

    lax.fori_loop(0, 8, place_rows, 0)

    def return_copy(i, kv, quad, device):
        cols = lanes_of(quad)
        return remote(sbuf.at[i, kv, :, cols], rbuf.at[i, kv, :, cols], ret_ss.at[i, kv, quad], ret_rs.at[i, kv, quad], device)

    def backward_quad(i, quad):
        t = tile_of(i)
        cols = lanes_of(quad)
        window = pl.ds(pl.multiple_of(t * TILE, TILE), WIN)
        n = i * QUADS + quad
        part = dout[:, cols].astype(F32)
        pairs = [part[:, :128], part[:, :128], part[:, 128:], part[:, 128:]]
        grads = spread([pairs[h] * rl_rows[n, h * TILE : (h + 1) * TILE, :] for h in range(4)])
        weights = probs[n]
        prob_grad = dot(vx[window, cols], grads, 1, 1)
        wide = weights.astype(F32)
        row_dot = jnp.sum(wide * prob_grad, axis=0, keepdims=True) * rl_lanes[n, 0:1, :]
        score_grad = (wide * (prob_grad - row_dot)).astype(BF16)
        keys = kx[window, cols]
        halves = []
        for half in range(2):
            side = slice(half * 128, half * 128 + 128)
            mixed = dot(score_grad[:, side], keys[:, side], 0, 0) * 0.125
            halves.append(jnp.where(left_half, mixed[:TILE], mixed[TILE:]))
        rows = pl.ds(pl.multiple_of(t * TILE, TILE), TILE)
        gq_s[rows, cols] = jnp.concatenate(halves, axis=1).astype(BF16)
        acc_k[window, cols] += dot(score_grad, query_block(t, quad), 1, 0)
        acc_v[window, cols] += dot(weights, grads, 1, 0)

        first = jnp.where(i % 2 == 0, TILE * (i // 2), EXT - TILE - TILE * (i // 2))
        done = pl.ds(pl.multiple_of(first, TILE), TILE)
        sbuf[i, 0, :, cols] = acc_k[done, cols].astype(BF16)
        sbuf[i, 1, :, cols] = acc_v[done, cols].astype(BF16)

        @pl.when((i % 2 == 0) & has_lower)
        def _():
            return_copy(i, 0, quad, lower).start()
            return_copy(i, 1, quad, lower).start()

        @pl.when((i % 2 == 1) & has_upper)
        def _():
            return_copy(i, 0, quad, upper).start()
            return_copy(i, 1, quad, upper).start()

    def backward_tile(i, carry):
        t = tile_of(i)

        def pass_on(quad, inner):
            far_copy(i, quad).wait_recv()
            fwd_copy(i, quad).start()
            return inner

        lax.fori_loop(0, QUADS, pass_on, 0)
        sib_copy(i).wait_recv()

        def arrived(quad, inner):
            fwd_copy(i, quad).wait_recv()
            return inner

        lax.fori_loop(0, QUADS, arrived, 0)
        cohort = att[:, i].reshape(4 * TILE, WIDTH)
        rows = pl.ds(pl.multiple_of(t * TILE, TILE), TILE)

        total = jnp.zeros((TILE, WIDTH), F32)
        pieces = []
        for b in range(4):
            cols = slice(b * 256, b * 256 + 256)
            forecast = dot(cohort, w_s[:, cols], 1, 0).astype(BF16).astype(F32)
            resident = forecast[:TILE]
            couples = slope(resident - forecast[TILE : 2 * TILE])
            couples += slope(resident - forecast[2 * TILE : 3 * TILE])
            couples += slope(resident - forecast[3 * TILE :])
            truth = obs[rows, cols].astype(F32)
            pieces.append((slope(resident - truth) - couples * (1.0 / 3.0)).astype(BF16))
        field_grad = jnp.concatenate(pieces, axis=1)
        dout[...] = dot(field_grad, w_s[...], 1, 1).astype(BF16)

        def step(quad, inner):
            backward_quad(i, quad)
            return inner

        lax.fori_loop(0, QUADS, step, 0)
        return carry

    lax.fori_loop(0, TILES, backward_tile, 0)

    copies_out = [pltpu.make_async_copy(gq_s, gq_hbm.at[0], out_sem.at[0])]
    copies_out[0].start()

    for block, slot in ((2, 0), (1, 1), (3, 2), (0, 3)):
        source_exists = has_upper if slot % 2 == 0 else has_lower
        source = upper if slot % 2 == 0 else lower
        rows = slice(block * TILE, block * TILE + TILE)
        inner_rows = slice(REACH + block * TILE, REACH + block * TILE + TILE)

        def finish(quad, carry, slot=slot, source_exists=source_exists, source=source, rows=rows, inner_rows=inner_rows):
            @pl.when(source_exists)
            def _():
                return_copy(slot, 0, quad, source).wait_recv()
                return_copy(slot, 1, quad, source).wait_recv()

            cols = lanes_of(quad)
            gk_s[rows, cols] = (acc_k[inner_rows, cols] + rbuf[slot, 0, :, cols].astype(F32)).astype(BF16)
            gv_s[rows, cols] = (acc_v[inner_rows, cols] + rbuf[slot, 1, :, cols].astype(F32)).astype(BF16)
            return carry

        lax.fori_loop(0, QUADS, finish, 0)
        pair = [
            pltpu.make_async_copy(gk_s.at[rows], gk_hbm.at[0, rows], out_sem.at[1 + 2 * block]),
            pltpu.make_async_copy(gv_s.at[rows], gv_hbm.at[0, rows], out_sem.at[2 + 2 * block]),
        ]
        for cp in pair:
            cp.start()
        copies_out += pair

    for step in range(4):
        w_sent(step)
    w_sib_out.wait_send()

    def sent(quad, carry):
        @pl.when(has_upper)
        def _():
            halo(0, 0, quad).wait_send()
            halo(0, 1, quad).wait_send()

        @pl.when(has_lower)
        def _():
            halo(1, 0, quad).wait_send()
            halo(1, 1, quad).wait_send()

        for i in range(TILES):
            far_copy(i, quad).wait_send()
            fwd_copy(i, quad).wait_send()

            @pl.when(has_lower if i % 2 == 0 else has_upper)
            def _(i=i):
                device = lower if i % 2 == 0 else upper
                return_copy(i, 0, quad, device).wait_send()
                return_copy(i, 1, quad, device).wait_send()

        return carry

    lax.fori_loop(0, QUADS, sent, 0)
    for i in range(TILES):
        sib_copy(i).wait_send()
    for cp in copies_out:
        cp.wait()


def body(query_states, key_states, value_states, observed, closing_projector):
    dma = pltpu.SemaphoreType.DMA
    hbm = pl.BlockSpec(memory_space=pl.ANY)
    grad = jax.ShapeDtypeStruct((1, ROWS, WIDTH), BF16)
    vmem = pltpu.VMEM
    return pl.pallas_call(
        kernel,
        out_shape=(grad, grad, grad),
        in_specs=[hbm, hbm, hbm, hbm, pl.BlockSpec(memory_space=pltpu.VMEM)],
        out_specs=(hbm, hbm, hbm),
        scratch_shapes=[
            vmem((ROWS, WIDTH), BF16),
            vmem((EXT, WIDTH), BF16),
            vmem((EXT, WIDTH), BF16),
            vmem((ROWS, WIDTH), BF16),
            vmem((16, 128), F32),
            vmem((512, 16, 128), BF16),
            vmem((8192, 128), F32),
            vmem((WIDTH, WIDTH), BF16),
            vmem((4, TILES, TILE, WIDTH), BF16),
            vmem((TILES * QUADS, WIN, LANES), BF16),
            vmem((TILES * QUADS, LANES, 128), F32),
            vmem((TILES * QUADS, 8, LANES), F32),
            vmem((TILES, WIN, LANES), F32),
            vmem((TILE, WIDTH), BF16),
            vmem((EXT, WIDTH), F32),
            vmem((EXT, WIDTH), F32),
            vmem((TILES, 2, TILE, WIDTH), BF16),
            vmem((TILES, 2, TILE, WIDTH), BF16),
            vmem((ROWS, WIDTH), BF16),
            vmem((ROWS, WIDTH), BF16),
            vmem((ROWS, WIDTH), BF16),
            dma((4,)),
            dma((2, 2, QUADS)), dma((2, 2, QUADS)),
            dma((3,)), dma((3,)),
            dma((3,)), dma((3,)),
            dma((3,)), dma((3,)),
            dma((3,)), dma((3,)),
            dma, dma,
            dma((TILES, QUADS)), dma((TILES, QUADS)),
            dma((TILES,)), dma((TILES,)),
            dma((TILES, QUADS)), dma((TILES, QUADS)),
            dma((TILES, 2, QUADS)), dma((TILES, 2, QUADS)),
            dma((9,)),
        ],
        compiler_params=pltpu.CompilerParams(
            collective_id=0, has_side_effects=True, vmem_limit_bytes=50 * 1024 * 1024
        ),
        name="window_backward",
    )(query_states, key_states, value_states, observed, closing_projector)


def solution(mesh):
    placed = (
        P("mem", "tok", None),
        P("mem", "tok", None),
        P("mem", "tok", None),
        P("tok", None),
        P(("tok", "mem"), None),
    )
    return jax.shard_map(
        body,
        mesh=mesh,
        in_specs=placed,
        out_specs=(P("mem", "tok", None), P("mem", "tok", None), P("mem", "tok", None)),
        check_vma=False,
    )
```

```python
import jax
import jax.numpy as jnp
from jax import lax
from jax.experimental import pallas as pl
from jax.experimental.pallas import tpu as pltpu
from jax.sharding import PartitionSpec as P

MESH = pl.DeviceIdType.MESH
F32 = jnp.float32
BF16 = jnp.bfloat16

TOK = 128
ROWS = 256
REACH = 128
WIDTH = 1024
HD = 64
TILE = 64
TILES = 4
WIN = TILE + 2 * REACH
LANES = 256
QUADS = 4
EXT = ROWS + 2 * REACH
BLOCKED = -1e30


def chip(x, y, z, c):
    return ((z % 8) * 16 + x * 4 + y, (z // 8) * 2 + c)


def dot(a, b, ca, cb):
    return lax.dot_general(a, b, (((ca,), (cb,)), ((), ())), preferred_element_type=F32)


def slope(d):
    return d * lax.rsqrt(d * d + 0.25)


def lanes_of(quad):
    return pl.ds(pl.multiple_of(quad * LANES, LANES), LANES)


def kernel(
    q_hbm, k_hbm, v_hbm, o_hbm, w_in,
    gq_hbm, gk_hbm, gv_hbm,
    q_s, kx, vx, obs, w_tmp, wg, wf, w_s, att, probs, rl_rows, rl_lanes, bias,
    dout, acc_k, acc_v, sbuf, rbuf, gq_s, gk_s, gv_s,
    load_sem, halo_ss, halo_rs, wz_ss, wz_rs, wy_ss, wy_rs, wx_ss, wx_rs, wc_ss, wc_rs,
    far_ss, far_rs, sib_ss, sib_rs, fwd_ss, fwd_rs, ret_ss, ret_rs, out_sem,
):
    tok = lax.axis_index("tok")
    mem = lax.axis_index("mem")
    x = (tok // 4) % 4
    y = tok % 4
    z = (mem // 2) * 8 + tok // 16
    c = mem % 2
    sibling = (tok, (mem // 2) * 2 + (1 - c))
    far = (tok, (mem + 2) % 4)
    lower = (tok - 1, mem)
    upper = (tok + 1, mem)
    has_lower = tok > 0
    has_upper = tok < TOK - 1

    def remote(src, dst, ss, rs, device):
        return pltpu.make_async_remote_copy(
            src_ref=src, dst_ref=dst, send_sem=ss, recv_sem=rs, device_id=device, device_id_type=MESH
        )

    barrier = pltpu.get_barrier_semaphore()

    def greet(device):
        pl.semaphore_signal(barrier, inc=1, device_id=device, device_id_type=MESH)

    greet(sibling)
    for d in range(1, 16):
        greet(chip(x, y, (z + d) % 16, c))
    for d in (1, 2, 3):
        greet(chip(x, (y + d) % 4, z, c))
        greet(chip((x + d) % 4, y, z, c))

    first = tok % 16 == 0

    @pl.when(has_lower)
    def _():
        greet(lower)

    @pl.when(has_upper)
    def _():
        greet(upper)

    own = pl.ds(REACH, ROWS)
    loads = [
        pltpu.make_async_copy(k_hbm.at[0], kx.at[own], load_sem.at[0]),
        pltpu.make_async_copy(q_hbm.at[0], q_s, load_sem.at[1]),
        pltpu.make_async_copy(v_hbm.at[0], vx.at[own], load_sem.at[2]),
        pltpu.make_async_copy(o_hbm, obs, load_sem.at[3]),
    ]
    for cp in loads:
        cp.start()

    mine = w_in[...].astype(F32)
    for r in range(2):
        for b in range(8):
            w_tmp[r * 8 + b : r * 8 + b + 1, :] = mine[r : r + 1, b * 128 : (b + 1) * 128]
    unit = ((c * 4 + x) * 4 + y) * 16 + z
    wg[unit] = w_tmp[...].astype(BF16)

    def one(flag):
        return jnp.where(flag, 1, 0)

    pl.semaphore_wait(
        barrier,
        22 + one(has_lower) + one(has_upper),
    )

    def halo_parts(side, kv, quad):
        ref = (kx, vx)[kv]
        source = pl.ds(ROWS, REACH) if side == 0 else pl.ds(REACH, REACH)
        target = pl.ds(0, REACH) if side == 0 else pl.ds(REACH + ROWS, REACH)
        return ref.at[source, lanes_of(quad)], ref.at[target, lanes_of(quad)]

    def halo(side, kv, quad):
        src, dst = halo_parts(side, kv, quad)
        return remote(
            src, dst, halo_ss.at[side, kv, quad], halo_rs.at[side, kv, quad], upper if side == 0 else lower
        )

    def start_halo(quad, carry):
        for kv in range(2):

            @pl.when(has_upper)
            def _(kv=kv):
                halo(0, kv, quad).start()

            @pl.when(has_lower)
            def _(kv=kv):
                halo(1, kv, quad).start()

        return carry

    def halos_sent():
        def step(quad, carry):
            for kv in range(2):

                @pl.when(has_upper)
                def _(kv=kv):
                    halo(0, kv, quad).wait_send()

                @pl.when(has_lower)
                def _(kv=kv):
                    halo(1, kv, quad).wait_send()

            return carry

        lax.fori_loop(0, QUADS, step, 0)

    def w_copy(first, count, ss, rs, device):
        block = wg.at[pl.ds(first, count)]
        return remote(block, block, ss, rs, device)

    def w_step(step, d, incoming):
        if step == 0:
            level = (z + 16 - d) % 16 if incoming else z
            return w_copy(
                ((c * 4 + x) * 4 + y) * 16 + level, 1, wz_ss.at[d - 1], wz_rs.at[d - 1],
                chip(x, y, (z + d) % 16, c),
            )
        if step == 1:
            column = (y + 4 - d) % 4 if incoming else y
            return w_copy(
                ((c * 4 + x) * 4 + column) * 16, 16, wy_ss.at[d - 1], wy_rs.at[d - 1],
                chip(x, (y + d) % 4, z, c),
            )
        column = (x + 4 - d) % 4 if incoming else x
        return w_copy(
            (c * 4 + column) * 64, 64, wx_ss.at[d - 1], wx_rs.at[d - 1], chip((x + d) % 4, y, z, c)
        )

    def w_offsets(step):
        return range(1, 16 if step == 0 else 4)

    def w_start(step):
        for d in w_offsets(step):
            w_step(step, d, False).start()

    def w_wait(step):
        for d in w_offsets(step):
            w_step(step, d, True).wait_recv()

    def w_sent(step):
        for d in w_offsets(step):
            w_step(step, d, False).wait_send()

    w_sib_out = w_copy(c * 256, 256, wc_ss, wc_rs, sibling)
    w_sib_in = w_copy((1 - c) * 256, 256, wc_ss, wc_rs, sibling)

    w_start(0)
    loads[0].wait()
    loads[2].wait()
    lax.fori_loop(0, QUADS, start_halo, 0)

    row = lax.broadcasted_iota(jnp.int32, (WIN, LANES), 0)
    query = lax.broadcasted_iota(jnp.int32, (WIN, LANES), 1) % TILE
    band = (row >= query) & (row <= query + 2 * REACH)
    for t in range(TILES):
        place = row + TILE * t
        lowest = jnp.where(has_lower, 0, REACH)
        highest = jnp.where(has_upper, EXT, REACH + ROWS)
        inside = (place >= lowest) & (place < highest)
        bias[t] = jnp.where(band & inside, 0.0, BLOCKED)

    def zero(i, carry):
        rows = pl.ds(pl.multiple_of(i * 32, 32), 32)
        acc_k[rows, :] = jnp.zeros((32, WIDTH), F32)
        acc_v[rows, :] = jnp.zeros((32, WIDTH), F32)
        return carry

    lax.fori_loop(0, EXT // 32, zero, 0)

    @pl.when(jnp.logical_not(has_lower))
    def _():
        kx[pl.ds(0, REACH), :] = jnp.zeros((REACH, WIDTH), BF16)
        vx[pl.ds(0, REACH), :] = jnp.zeros((REACH, WIDTH), BF16)
        for slot in (1, 3):
            rbuf[slot] = jnp.zeros((2, TILE, WIDTH), BF16)

    @pl.when(jnp.logical_not(has_upper))
    def _():
        kx[pl.ds(REACH + ROWS, REACH), :] = jnp.zeros((REACH, WIDTH), BF16)
        vx[pl.ds(REACH + ROWS, REACH), :] = jnp.zeros((REACH, WIDTH), BF16)
        for slot in (0, 2):
            rbuf[slot] = jnp.zeros((2, TILE, WIDTH), BF16)

    loads[1].wait()
    loads[3].wait()
    left_half = lax.broadcasted_iota(jnp.int32, (TILE, 128), 1) < HD

    def spread(pairs):
        none = jnp.zeros((TILE, 128), F32)
        rows = []
        for h in range(4):
            keep = left_half if h % 2 == 0 else jnp.logical_not(left_half)
            part = jnp.where(keep, pairs[h], 0.0)
            rows.append(jnp.concatenate([part, none] if h < 2 else [none, part], axis=1))
        return jnp.concatenate(rows, axis=0).astype(BF16)

    mirrored = jnp.where(first, 1, 0)

    def tile_of(i):
        t = i + (i // 2) * (5 - 2 * i)
        return t + mirrored * (3 - 2 * t)

    def slot_of(i):
        slot = (i % 2) * 2 + i // 2
        return slot + mirrored * (1 - 2 * (slot % 2))

    def query_block(t, quad):
        rows = pl.ds(pl.multiple_of(t * TILE, TILE), TILE)
        part = q_s[rows, lanes_of(quad)].astype(F32) * 0.125
        return spread([part[:, :128], part[:, :128], part[:, 128:], part[:, 128:]])

    def far_copy(i, quad):
        cols = lanes_of(quad)
        return remote(att.at[0, i, :, cols], att.at[2, i, :, cols], far_ss.at[i, quad], far_rs.at[i, quad], far)

    def fwd_copy(i, quad):
        cols = lanes_of(quad)
        return remote(att.at[2, i, :, cols], att.at[3, i, :, cols], fwd_ss.at[i, quad], fwd_rs.at[i, quad], sibling)

    def sib_copy(i):
        return remote(att.at[0, i], att.at[1, i], sib_ss.at[i], sib_rs.at[i], sibling)

    ones = jnp.ones((WIN, 128), BF16)

    def forward_quad(i, quad):
        t = tile_of(i)

        @pl.when((slot_of(i) == 0) & has_lower)
        def _():
            halo(0, 0, quad).wait_recv()
            halo(0, 1, quad).wait_recv()

        @pl.when((slot_of(i) == 1) & has_upper)
        def _():
            halo(1, 0, quad).wait_recv()
            halo(1, 1, quad).wait_recv()

        cols = lanes_of(quad)
        window = pl.ds(pl.multiple_of(t * TILE, TILE), WIN)
        scores = dot(kx[window, cols], query_block(t, quad), 1, 1) + bias[t]
        top = jnp.max(scores, axis=0, keepdims=True)
        weights = jnp.exp(scores - top).astype(BF16)
        total = jnp.sum(weights.astype(F32), axis=0, keepdims=True)
        n = i * QUADS + quad
        probs[n] = weights
        rl_lanes[n] = jnp.broadcast_to(1.0 / total, (8, LANES))
        values = vx[window, cols]
        halves = []
        for half in range(2):
            part = slice(half * 128, half * 128 + 128)
            rhs = jnp.concatenate([values[:, part], ones], axis=1)
            mixed = dot(weights[:, part], rhs, 0, 0)
            inverse = 1.0 / mixed[:, 128:]
            rl_rows[n, pl.ds(half * 128, 128), :] = inverse
            mixed = mixed[:, :128] * inverse
            halves.append(jnp.where(left_half, mixed[:TILE], mixed[TILE:]))
        att[0, i, :, cols] = jnp.concatenate(halves, axis=1).astype(BF16)
        far_copy(i, quad).start()

    def forward_tile(i, carry):
        def step(quad, inner):
            forward_quad(i, quad)
            return inner

        lax.fori_loop(0, QUADS, step, 0)
        sib_copy(i).start()

        @pl.when(i == 0)
        def _():
            w_wait(0)
            w_start(1)

        @pl.when(i == 1)
        def _():
            w_wait(1)
            w_start(2)

        return carry

    lax.fori_loop(0, TILES, forward_tile, 0)

    def pass_on(i):
        def step(quad, inner):
            far_copy(i, quad).wait_recv()
            fwd_copy(i, quad).start()
            return inner

        lax.fori_loop(0, QUADS, step, 0)

    pass_on(0)
    w_wait(2)
    w_sib_out.start()
    w_sib_in.wait_recv()

    def place_units(n, carry):
        for level in range(16):
            d = (level % 8) * 64 + (n % 16) * 4 + (level // 8) * 2 + n // 16
            wf[pl.ds(pl.multiple_of(d * 16, 16), 16), :] = wg[n * 16 + level].astype(F32)
        return carry

    lax.fori_loop(0, 32, place_units, 0)

    def place_rows(n, carry):
        rows = pl.ds(pl.multiple_of(n * 128, 128), 128)
        for b in range(8):
            part = wf[pl.ds(n * 1024 + b, 128, stride=8), :]
            w_s[rows, b * 128 : (b + 1) * 128] = part.astype(BF16)
        return carry

    lax.fori_loop(0, 8, place_rows, 0)

    def return_copy(i, kv, quad, device):
        cols = lanes_of(quad)
        return remote(sbuf.at[i, kv, :, cols], rbuf.at[i, kv, :, cols], ret_ss.at[i, kv, quad], ret_rs.at[i, kv, quad], device)

    def start_return(slot, quad):
        for kv in range(2):

            @pl.when((slot % 2 == 0) & has_lower)
            def _(kv=kv):
                return_copy(slot, kv, quad, lower).start()

            @pl.when((slot % 2 == 1) & has_upper)
            def _(kv=kv):
                return_copy(slot, kv, quad, upper).start()

    def backward_quad(i, quad):
        t = tile_of(i)
        cols = lanes_of(quad)
        window = pl.ds(pl.multiple_of(t * TILE, TILE), WIN)
        n = i * QUADS + quad
        part = dout[:, cols].astype(F32)
        pairs = [part[:, :128], part[:, :128], part[:, 128:], part[:, 128:]]
        grads = spread([pairs[h] * rl_rows[n, h * TILE : (h + 1) * TILE, :] for h in range(4)])
        weights = probs[n]
        prob_grad = dot(vx[window, cols], grads, 1, 1)
        wide = weights.astype(F32)
        row_dot = jnp.sum(wide * prob_grad, axis=0, keepdims=True) * rl_lanes[n, 0:1, :]
        score_grad = (wide * (prob_grad - row_dot)).astype(BF16)
        keys = kx[window, cols]
        halves = []
        for half in range(2):
            side = slice(half * 128, half * 128 + 128)
            mixed = dot(score_grad[:, side], keys[:, side], 0, 0) * 0.125
            halves.append(jnp.where(left_half, mixed[:TILE], mixed[TILE:]))
        rows = pl.ds(pl.multiple_of(t * TILE, TILE), TILE)
        gq_s[rows, cols] = jnp.concatenate(halves, axis=1).astype(BF16)
        acc_k[window, cols] += dot(score_grad, query_block(t, quad), 1, 0)
        acc_v[window, cols] += dot(weights, grads, 1, 0)

        slot = slot_of(i)
        first_row = jnp.where(slot % 2 == 0, TILE * (slot // 2), EXT - TILE - TILE * (slot // 2))
        done = pl.ds(pl.multiple_of(first_row, TILE), TILE)
        sbuf[slot, 0, :, cols] = acc_k[done, cols].astype(BF16)
        sbuf[slot, 1, :, cols] = acc_v[done, cols].astype(BF16)
        start_return(slot, quad)

    def backward_tile(i, carry):
        t = tile_of(i)

        @pl.when(i > 0)
        def _():
            pass_on(i)

        sib_copy(i).wait_recv()

        def arrived(quad, inner):
            fwd_copy(i, quad).wait_recv()
            return inner

        lax.fori_loop(0, QUADS, arrived, 0)

        cohort = att[:, i].reshape(4 * TILE, WIDTH)
        rows = pl.ds(pl.multiple_of(t * TILE, TILE), TILE)

        total = jnp.zeros((TILE, WIDTH), F32)
        pieces = []
        for b in range(4):
            cols = slice(b * 256, b * 256 + 256)
            forecast = dot(cohort, w_s[:, cols], 1, 0).astype(BF16).astype(F32)
            resident = forecast[:TILE]
            couples = slope(resident - forecast[TILE : 2 * TILE])
            couples += slope(resident - forecast[2 * TILE : 3 * TILE])
            couples += slope(resident - forecast[3 * TILE :])
            truth = obs[rows, cols].astype(F32)
            pieces.append((slope(resident - truth) - couples * (1.0 / 3.0)).astype(BF16))
        field_grad = jnp.concatenate(pieces, axis=1)
        dout[...] = dot(field_grad, w_s[...], 1, 1).astype(BF16)

        def step(quad, inner):
            backward_quad(i, quad)
            return inner

        lax.fori_loop(0, QUADS, step, 0)

        return carry

    lax.fori_loop(0, TILES, backward_tile, 0)

    copies_out = [pltpu.make_async_copy(gq_s, gq_hbm.at[0], out_sem.at[0])]
    copies_out[0].start()

    for block, slot in ((2, 0), (1, 1), (3, 2), (0, 3)):
        source_exists = has_upper if slot % 2 == 0 else has_lower
        source = upper if slot % 2 == 0 else lower
        rows = slice(block * TILE, block * TILE + TILE)
        inner_rows = slice(REACH + block * TILE, REACH + block * TILE + TILE)

        def finish(quad, carry, slot=slot, source_exists=source_exists, source=source, rows=rows, inner_rows=inner_rows):
            @pl.when(source_exists)
            def _():
                return_copy(slot, 0, quad, source).wait_recv()
                return_copy(slot, 1, quad, source).wait_recv()

            cols = lanes_of(quad)
            gk_s[rows, cols] = (acc_k[inner_rows, cols] + rbuf[slot, 0, :, cols].astype(F32)).astype(BF16)
            gv_s[rows, cols] = (acc_v[inner_rows, cols] + rbuf[slot, 1, :, cols].astype(F32)).astype(BF16)
            return carry

        lax.fori_loop(0, QUADS, finish, 0)
        pair = [
            pltpu.make_async_copy(gk_s.at[rows], gk_hbm.at[0, rows], out_sem.at[1 + 2 * block]),
            pltpu.make_async_copy(gv_s.at[rows], gv_hbm.at[0, rows], out_sem.at[2 + 2 * block]),
        ]
        for cp in pair:
            cp.start()
        copies_out += pair

    for step in range(3):
        w_sent(step)
    w_sib_out.wait_send()

    halos_sent()

    def sent(quad, carry):
        for i in range(TILES):
            far_copy(i, quad).wait_send()
            fwd_copy(i, quad).wait_send()

            @pl.when(has_lower if i % 2 == 0 else has_upper)
            def _(i=i):
                device = lower if i % 2 == 0 else upper
                return_copy(i, 0, quad, device).wait_send()
                return_copy(i, 1, quad, device).wait_send()

        return carry

    lax.fori_loop(0, QUADS, sent, 0)
    for i in range(TILES):
        sib_copy(i).wait_send()

    for cp in copies_out:
        cp.wait()


def body(query_states, key_states, value_states, observed, closing_projector):
    dma = pltpu.SemaphoreType.DMA
    hbm = pl.BlockSpec(memory_space=pltpu.HBM)
    grad = jax.ShapeDtypeStruct((1, ROWS, WIDTH), BF16)
    vmem = pltpu.VMEM
    return pl.pallas_call(
        kernel,
        out_shape=(grad, grad, grad),
        in_specs=[hbm] * 4 + [pl.BlockSpec(memory_space=pltpu.VMEM)],
        out_specs=(pl.BlockSpec(memory_space=pl.ANY),) * 3,
        scratch_shapes=[
            vmem((ROWS, WIDTH), BF16),
            vmem((EXT, WIDTH), BF16),
            vmem((EXT, WIDTH), BF16),
            vmem((ROWS, WIDTH), BF16),
            vmem((16, 128), F32),
            vmem((512, 16, 128), BF16),
            vmem((8192, 128), F32),
            vmem((WIDTH, WIDTH), BF16),
            vmem((4, TILES, TILE, WIDTH), BF16),
            vmem((TILES * QUADS, WIN, LANES), BF16),
            vmem((TILES * QUADS, LANES, 128), F32),
            vmem((TILES * QUADS, 8, LANES), F32),
            vmem((TILES, WIN, LANES), F32),
            vmem((TILE, WIDTH), BF16),
            vmem((EXT, WIDTH), F32),
            vmem((EXT, WIDTH), F32),
            vmem((TILES, 2, TILE, WIDTH), BF16),
            vmem((TILES, 2, TILE, WIDTH), BF16),
            vmem((ROWS, WIDTH), BF16),
            vmem((ROWS, WIDTH), BF16),
            vmem((ROWS, WIDTH), BF16),
            dma((4,)),
            dma((2, 2, QUADS)), dma((2, 2, QUADS)),
            dma((15,)), dma((15,)),
            dma((3,)), dma((3,)),
            dma((3,)), dma((3,)),
            dma, dma,
            dma((TILES, QUADS)), dma((TILES, QUADS)),
            dma((TILES,)), dma((TILES,)),
            dma((TILES, QUADS)), dma((TILES, QUADS)),
            dma((TILES, 2, QUADS)), dma((TILES, 2, QUADS)),
            dma((9,)),
        ],
        compiler_params=pltpu.CompilerParams(
            collective_id=0, has_side_effects=True, vmem_limit_bytes=56 * 1024 * 1024
        ),
        name="window_backward",
    )(query_states, key_states, value_states, observed, closing_projector)


def solution(mesh):
    placed = (
        P("mem", "tok", None),
        P("mem", "tok", None),
        P("mem", "tok", None),
        P("tok", None),
        P(("tok", "mem"), None),
    )
    return jax.shard_map(
        body,
        mesh=mesh,
        in_specs=placed,
        out_specs=(P("mem", "tok", None), P("mem", "tok", None), P("mem", "tok", None)),
        check_vma=False,
    )
```

```python
import jax
import jax.numpy as jnp
from jax import lax
from jax.experimental import pallas as pl
from jax.experimental.pallas import tpu as pltpu
from jax.sharding import PartitionSpec as P

MESH = pl.DeviceIdType.MESH
F32 = jnp.float32
BF16 = jnp.bfloat16

TOK = 128
ROWS = 256
REACH = 128
WIDTH = 1024
HD = 64
TILE = 64
TILES = 4
WIN = TILE + 2 * REACH
LANES = 256
QUADS = 4
EXT = ROWS + 2 * REACH
BLOCKED = -1e30


def chip(x, y, z, c):
    return ((z % 8) * 16 + x * 4 + y, (z // 8) * 2 + c)


def dot(a, b, ca, cb):
    return lax.dot_general(a, b, (((ca,), (cb,)), ((), ())), preferred_element_type=F32)


def slope(d):
    return d * lax.rsqrt(d * d + 0.25)


def lanes_of(quad):
    return pl.ds(pl.multiple_of(quad * LANES, LANES), LANES)


def kernel(
    q_hbm, k_hbm, v_hbm, o_hbm, w_in,
    gq_hbm, gk_hbm, gv_hbm,
    q_s, kx, vx, obs, w_tmp, wg, wf, w_s, att, probs, rl_rows, rl_lanes, bias,
    dout, acc_k, acc_v, sbuf, rbuf, gq_s, gk_s, gv_s,
    load_sem, halo_ss, halo_rs, wz_ss, wz_rs, wy_ss, wy_rs, wx_ss, wx_rs, wc_ss, wc_rs,
    far_ss, far_rs, sib_ss, sib_rs, fwd_ss, fwd_rs, ret_ss, ret_rs, out_sem,
):
    tok = lax.axis_index("tok")
    mem = lax.axis_index("mem")
    x = (tok // 4) % 4
    y = tok % 4
    z = (mem // 2) * 8 + tok // 16
    c = mem % 2
    sibling = (tok, (mem // 2) * 2 + (1 - c))
    far = (tok, (mem + 2) % 4)
    lower = (tok - 1, mem)
    upper = (tok + 1, mem)
    has_lower = tok > 0
    has_upper = tok < TOK - 1

    def remote(src, dst, ss, rs, device):
        return pltpu.make_async_remote_copy(
            src_ref=src, dst_ref=dst, send_sem=ss, recv_sem=rs, device_id=device, device_id_type=MESH
        )

    barrier = pltpu.get_barrier_semaphore()

    def greet(device):
        pl.semaphore_signal(barrier, inc=1, device_id=device, device_id_type=MESH)

    greet(sibling)
    for d in range(1, 16):
        greet(chip(x, y, (z + d) % 16, c))
    for d in (1, 2, 3):
        greet(chip(x, (y + d) % 4, z, c))
        greet(chip((x + d) % 4, y, z, c))

    first = tok % 16 == 0

    @pl.when(has_lower)
    def _():
        greet(lower)

    @pl.when(has_upper)
    def _():
        greet(upper)

    own = pl.ds(REACH, ROWS)
    loads = [
        pltpu.make_async_copy(k_hbm.at[0], kx.at[own], load_sem.at[0]),
        pltpu.make_async_copy(q_hbm.at[0], q_s, load_sem.at[1]),
        pltpu.make_async_copy(v_hbm.at[0], vx.at[own], load_sem.at[2]),
        pltpu.make_async_copy(o_hbm, obs, load_sem.at[3]),
    ]
    for cp in loads:
        cp.start()

    mine = w_in[...].astype(F32)
    for r in range(2):
        for b in range(8):
            w_tmp[r * 8 + b : r * 8 + b + 1, :] = mine[r : r + 1, b * 128 : (b + 1) * 128]
    unit = ((c * 4 + x) * 4 + y) * 16 + z
    wg[unit] = w_tmp[...].astype(BF16)

    def one(flag):
        return jnp.where(flag, 1, 0)

    pl.semaphore_wait(
        barrier,
        22 + one(has_lower) + one(has_upper),
    )

    def halo_parts(side, kv, quad):
        ref = (kx, vx)[kv]
        source = pl.ds(ROWS, REACH) if side == 0 else pl.ds(REACH, REACH)
        target = pl.ds(0, REACH) if side == 0 else pl.ds(REACH + ROWS, REACH)
        return ref.at[source, lanes_of(quad)], ref.at[target, lanes_of(quad)]

    def halo(side, kv, quad):
        src, dst = halo_parts(side, kv, quad)
        return remote(
            src, dst, halo_ss.at[side, kv, quad], halo_rs.at[side, kv, quad], upper if side == 0 else lower
        )

    def start_halo(quad, carry):
        for kv in range(2):

            @pl.when(has_upper)
            def _(kv=kv):
                halo(0, kv, quad).start()

            @pl.when(has_lower)
            def _(kv=kv):
                halo(1, kv, quad).start()

        return carry

    def halos_sent():
        def step(quad, carry):
            for kv in range(2):

                @pl.when(has_upper)
                def _(kv=kv):
                    halo(0, kv, quad).wait_send()

                @pl.when(has_lower)
                def _(kv=kv):
                    halo(1, kv, quad).wait_send()

            return carry

        lax.fori_loop(0, QUADS, step, 0)

    def w_copy(first, count, ss, rs, device):
        block = wg.at[pl.ds(first, count)]
        return remote(block, block, ss, rs, device)

    def w_step(step, d, incoming):
        if step == 0:
            level = (z + 16 - d) % 16 if incoming else z
            return w_copy(
                ((c * 4 + x) * 4 + y) * 16 + level, 1, wz_ss.at[d - 1], wz_rs.at[d - 1],
                chip(x, y, (z + d) % 16, c),
            )
        if step == 1:
            column = (y + 4 - d) % 4 if incoming else y
            return w_copy(
                ((c * 4 + x) * 4 + column) * 16, 16, wy_ss.at[d - 1], wy_rs.at[d - 1],
                chip(x, (y + d) % 4, z, c),
            )
        column = (x + 4 - d) % 4 if incoming else x
        return w_copy(
            (c * 4 + column) * 64, 64, wx_ss.at[d - 1], wx_rs.at[d - 1], chip((x + d) % 4, y, z, c)
        )

    def w_offsets(step):
        return range(1, 16 if step == 0 else 4)

    def w_start(step):
        for d in w_offsets(step):
            w_step(step, d, False).start()

    def w_wait(step):
        for d in w_offsets(step):
            w_step(step, d, True).wait_recv()

    def w_sent(step):
        for d in w_offsets(step):
            w_step(step, d, False).wait_send()

    w_sib_out = w_copy(c * 256, 256, wc_ss, wc_rs, sibling)
    w_sib_in = w_copy((1 - c) * 256, 256, wc_ss, wc_rs, sibling)

    w_start(0)
    loads[0].wait()
    loads[2].wait()
    lax.fori_loop(0, QUADS, start_halo, 0)

    row = lax.broadcasted_iota(jnp.int32, (WIN, LANES), 0)
    query = lax.broadcasted_iota(jnp.int32, (WIN, LANES), 1) % TILE
    band = (row >= query) & (row <= query + 2 * REACH)
    for t in range(TILES):
        place = row + TILE * t
        lowest = jnp.where(has_lower, 0, REACH)
        highest = jnp.where(has_upper, EXT, REACH + ROWS)
        inside = (place >= lowest) & (place < highest)
        bias[t] = jnp.where(band & inside, 0.0, BLOCKED)

    def zero(i, carry):
        rows = pl.ds(pl.multiple_of(i * 32, 32), 32)
        acc_k[rows, :] = jnp.zeros((32, WIDTH), F32)
        acc_v[rows, :] = jnp.zeros((32, WIDTH), F32)
        return carry

    lax.fori_loop(0, EXT // 32, zero, 0)

    @pl.when(jnp.logical_not(has_lower))
    def _():
        kx[pl.ds(0, REACH), :] = jnp.zeros((REACH, WIDTH), BF16)
        vx[pl.ds(0, REACH), :] = jnp.zeros((REACH, WIDTH), BF16)
        for slot in (1, 3):
            rbuf[slot] = jnp.zeros((2, TILE, WIDTH), BF16)

    @pl.when(jnp.logical_not(has_upper))
    def _():
        kx[pl.ds(REACH + ROWS, REACH), :] = jnp.zeros((REACH, WIDTH), BF16)
        vx[pl.ds(REACH + ROWS, REACH), :] = jnp.zeros((REACH, WIDTH), BF16)
        for slot in (0, 2):
            rbuf[slot] = jnp.zeros((2, TILE, WIDTH), BF16)

    loads[1].wait()
    loads[3].wait()
    left_half = lax.broadcasted_iota(jnp.int32, (TILE, 128), 1) < HD

    def spread(pairs):
        none = jnp.zeros((TILE, 128), F32)
        rows = []
        for h in range(4):
            keep = left_half if h % 2 == 0 else jnp.logical_not(left_half)
            part = jnp.where(keep, pairs[h], 0.0)
            rows.append(jnp.concatenate([part, none] if h < 2 else [none, part], axis=1))
        return jnp.concatenate(rows, axis=0).astype(BF16)

    mirrored = jnp.where(first, 1, 0)

    def tile_of(i):
        t = i + (i // 2) * (5 - 2 * i)
        return t + mirrored * (3 - 2 * t)

    def slot_of(i):
        slot = (i % 2) * 2 + i // 2
        return slot + mirrored * (1 - 2 * (slot % 2))

    def query_block(t, quad):
        rows = pl.ds(pl.multiple_of(t * TILE, TILE), TILE)
        part = q_s[rows, lanes_of(quad)].astype(F32) * 0.125
        return spread([part[:, :128], part[:, :128], part[:, 128:], part[:, 128:]])

    def far_copy(i, quad):
        cols = lanes_of(quad)
        return remote(att.at[0, i, :, cols], att.at[2, i, :, cols], far_ss.at[i, quad], far_rs.at[i, quad], far)

    def fwd_copy(i, quad):
        cols = lanes_of(quad)
        return remote(att.at[2, i, :, cols], att.at[3, i, :, cols], fwd_ss.at[i, quad], fwd_rs.at[i, quad], sibling)

    def sib_copy(i):
        return remote(att.at[0, i], att.at[1, i], sib_ss.at[i], sib_rs.at[i], sibling)

    ones = jnp.ones((WIN, 128), BF16)

    def forward_quad(i, quad):
        t = tile_of(i)

        @pl.when((slot_of(i) == 0) & has_lower)
        def _():
            halo(0, 0, quad).wait_recv()
            halo(0, 1, quad).wait_recv()

        @pl.when((slot_of(i) == 1) & has_upper)
        def _():
            halo(1, 0, quad).wait_recv()
            halo(1, 1, quad).wait_recv()

        cols = lanes_of(quad)
        window = pl.ds(pl.multiple_of(t * TILE, TILE), WIN)
        scores = dot(kx[window, cols], query_block(t, quad), 1, 1) + bias[t]
        top = jnp.max(scores, axis=0, keepdims=True)
        weights = jnp.exp(scores - top).astype(BF16)
        total = jnp.sum(weights.astype(F32), axis=0, keepdims=True)
        n = i * QUADS + quad
        probs[n] = weights
        rl_lanes[n] = jnp.broadcast_to(1.0 / total, (8, LANES))
        values = vx[window, cols]
        halves = []
        for half in range(2):
            part = slice(half * 128, half * 128 + 128)
            rhs = jnp.concatenate([values[:, part], ones], axis=1)
            mixed = dot(weights[:, part], rhs, 0, 0)
            inverse = 1.0 / mixed[:, 128:]
            rl_rows[n, pl.ds(half * 128, 128), :] = inverse
            mixed = mixed[:, :128] * inverse
            halves.append(jnp.where(left_half, mixed[:TILE], mixed[TILE:]))
        att[0, i, :, cols] = jnp.concatenate(halves, axis=1).astype(BF16)
        far_copy(i, quad).start()

    def forward_tile(i, carry):
        def step(quad, inner):
            forward_quad(i, quad)
            return inner

        lax.fori_loop(0, QUADS, step, 0)
        sib_copy(i).start()

        @pl.when(i == 0)
        def _():
            w_wait(0)
            w_start(1)

        @pl.when(i == 1)
        def _():
            w_wait(1)
            w_start(2)

        return carry

    lax.fori_loop(0, TILES, forward_tile, 0)

    def pass_on(i):
        def step(quad, inner):
            far_copy(i, quad).wait_recv()
            fwd_copy(i, quad).start()
            return inner

        lax.fori_loop(0, QUADS, step, 0)

    pass_on(0)
    w_wait(2)
    w_sib_out.start()
    w_sib_in.wait_recv()

    def place_units(n, carry):
        for level in range(16):
            d = (level % 8) * 64 + (n % 16) * 4 + (level // 8) * 2 + n // 16
            wf[pl.ds(pl.multiple_of(d * 16, 16), 16), :] = wg[n * 16 + level].astype(F32)
        return carry

    lax.fori_loop(0, 32, place_units, 0)

    def place_rows(n, carry):
        rows = pl.ds(pl.multiple_of(n * 128, 128), 128)
        for b in range(8):
            part = wf[pl.ds(n * 1024 + b, 128, stride=8), :]
            w_s[rows, b * 128 : (b + 1) * 128] = part.astype(BF16)
        return carry

    lax.fori_loop(0, 8, place_rows, 0)

    def return_copy(i, kv, quad, device):
        cols = lanes_of(quad)
        return remote(sbuf.at[i, kv, :, cols], rbuf.at[i, kv, :, cols], ret_ss.at[i, kv, quad], ret_rs.at[i, kv, quad], device)

    def start_return(slot, quad):
        for kv in range(2):

            @pl.when((slot % 2 == 0) & has_lower)
            def _(kv=kv):
                return_copy(slot, kv, quad, lower).start()

            @pl.when((slot % 2 == 1) & has_upper)
            def _(kv=kv):
                return_copy(slot, kv, quad, upper).start()

    def backward_quad(i, quad):
        t = tile_of(i)
        cols = lanes_of(quad)
        window = pl.ds(pl.multiple_of(t * TILE, TILE), WIN)
        n = i * QUADS + quad
        part = dout[:, cols].astype(F32)
        pairs = [part[:, :128], part[:, :128], part[:, 128:], part[:, 128:]]
        grads = spread([pairs[h] * rl_rows[n, h * TILE : (h + 1) * TILE, :] for h in range(4)])
        weights = probs[n]
        prob_grad = dot(vx[window, cols], grads, 1, 1)
        wide = weights.astype(F32)
        row_dot = jnp.sum(wide * prob_grad, axis=0, keepdims=True) * rl_lanes[n, 0:1, :]
        score_grad = (wide * (prob_grad - row_dot)).astype(BF16)
        acc_k[window, cols] += dot(score_grad, query_block(t, quad), 1, 0)
        acc_v[window, cols] += dot(weights, grads, 1, 0)

        slot = slot_of(i)
        first_row = jnp.where(slot % 2 == 0, TILE * (slot // 2), EXT - TILE - TILE * (slot // 2))
        done = pl.ds(pl.multiple_of(first_row, TILE), TILE)
        sbuf[slot, 0, :, cols] = acc_k[done, cols].astype(BF16)
        sbuf[slot, 1, :, cols] = acc_v[done, cols].astype(BF16)
        start_return(slot, quad)

        keys = kx[window, cols]
        halves = []
        for half in range(2):
            side = slice(half * 128, half * 128 + 128)
            mixed = dot(score_grad[:, side], keys[:, side], 0, 0) * 0.125
            halves.append(jnp.where(left_half, mixed[:TILE], mixed[TILE:]))
        rows = pl.ds(pl.multiple_of(t * TILE, TILE), TILE)
        gq_s[rows, cols] = jnp.concatenate(halves, axis=1).astype(BF16)

    def backward_tile(i, carry):
        t = tile_of(i)

        @pl.when(i > 0)
        def _():
            pass_on(i)

        sib_copy(i).wait_recv()

        def arrived(quad, inner):
            fwd_copy(i, quad).wait_recv()
            return inner

        lax.fori_loop(0, QUADS, arrived, 0)

        cohort = att[:, i].reshape(4 * TILE, WIDTH)
        rows = pl.ds(pl.multiple_of(t * TILE, TILE), TILE)

        total = jnp.zeros((TILE, WIDTH), F32)
        pieces = []
        for b in range(4):
            cols = slice(b * 256, b * 256 + 256)
            forecast = dot(cohort, w_s[:, cols], 1, 0).astype(BF16).astype(F32)
            resident = forecast[:TILE]
            couples = slope(resident - forecast[TILE : 2 * TILE])
            couples += slope(resident - forecast[2 * TILE : 3 * TILE])
            couples += slope(resident - forecast[3 * TILE :])
            truth = obs[rows, cols].astype(F32)
            pieces.append((slope(resident - truth) - couples * (1.0 / 3.0)).astype(BF16))
        field_grad = jnp.concatenate(pieces, axis=1)
        dout[...] = dot(field_grad, w_s[...], 1, 1).astype(BF16)

        def step(quad, inner):
            backward_quad(i, quad)
            return inner

        lax.fori_loop(0, QUADS, step, 0, unroll=2)

        return carry

    lax.fori_loop(0, TILES, backward_tile, 0)

    copies_out = [pltpu.make_async_copy(gq_s, gq_hbm.at[0], out_sem.at[0])]
    copies_out[0].start()

    for block, slot in ((2, 0), (1, 1), (3, 2), (0, 3)):
        source_exists = has_upper if slot % 2 == 0 else has_lower
        source = upper if slot % 2 == 0 else lower
        rows = slice(block * TILE, block * TILE + TILE)
        inner_rows = slice(REACH + block * TILE, REACH + block * TILE + TILE)

        def finish(quad, carry, slot=slot, source_exists=source_exists, source=source, rows=rows, inner_rows=inner_rows):
            @pl.when(source_exists)
            def _():
                return_copy(slot, 0, quad, source).wait_recv()
                return_copy(slot, 1, quad, source).wait_recv()

            cols = lanes_of(quad)
            gk_s[rows, cols] = (acc_k[inner_rows, cols] + rbuf[slot, 0, :, cols].astype(F32)).astype(BF16)
            gv_s[rows, cols] = (acc_v[inner_rows, cols] + rbuf[slot, 1, :, cols].astype(F32)).astype(BF16)
            return carry

        lax.fori_loop(0, QUADS, finish, 0)
        pair = [
            pltpu.make_async_copy(gk_s.at[rows], gk_hbm.at[0, rows], out_sem.at[1 + 2 * block]),
            pltpu.make_async_copy(gv_s.at[rows], gv_hbm.at[0, rows], out_sem.at[2 + 2 * block]),
        ]
        for cp in pair:
            cp.start()
        copies_out += pair

    for step in range(3):
        w_sent(step)
    w_sib_out.wait_send()

    halos_sent()

    def sent(quad, carry):
        for i in range(TILES):
            far_copy(i, quad).wait_send()
            fwd_copy(i, quad).wait_send()

            @pl.when(has_lower if i % 2 == 0 else has_upper)
            def _(i=i):
                device = lower if i % 2 == 0 else upper
                return_copy(i, 0, quad, device).wait_send()
                return_copy(i, 1, quad, device).wait_send()

        return carry

    lax.fori_loop(0, QUADS, sent, 0)
    for i in range(TILES):
        sib_copy(i).wait_send()

    for cp in copies_out:
        cp.wait()


def body(query_states, key_states, value_states, observed, closing_projector):
    dma = pltpu.SemaphoreType.DMA
    hbm = pl.BlockSpec(memory_space=pltpu.HBM)
    grad = jax.ShapeDtypeStruct((1, ROWS, WIDTH), BF16)
    vmem = pltpu.VMEM
    return pl.pallas_call(
        kernel,
        out_shape=(grad, grad, grad),
        in_specs=[hbm] * 4 + [pl.BlockSpec(memory_space=pltpu.VMEM)],
        out_specs=(pl.BlockSpec(memory_space=pl.ANY),) * 3,
        scratch_shapes=[
            vmem((ROWS, WIDTH), BF16),
            vmem((EXT, WIDTH), BF16),
            vmem((EXT, WIDTH), BF16),
            vmem((ROWS, WIDTH), BF16),
            vmem((16, 128), F32),
            vmem((512, 16, 128), BF16),
            vmem((8192, 128), F32),
            vmem((WIDTH, WIDTH), BF16),
            vmem((4, TILES, TILE, WIDTH), BF16),
            vmem((TILES * QUADS, WIN, LANES), BF16),
            vmem((TILES * QUADS, LANES, 128), F32),
            vmem((TILES * QUADS, 8, LANES), F32),
            vmem((TILES, WIN, LANES), F32),
            vmem((TILE, WIDTH), BF16),
            vmem((EXT, WIDTH), F32),
            vmem((EXT, WIDTH), F32),
            vmem((TILES, 2, TILE, WIDTH), BF16),
            vmem((TILES, 2, TILE, WIDTH), BF16),
            vmem((ROWS, WIDTH), BF16),
            vmem((ROWS, WIDTH), BF16),
            vmem((ROWS, WIDTH), BF16),
            dma((4,)),
            dma((2, 2, QUADS)), dma((2, 2, QUADS)),
            dma((15,)), dma((15,)),
            dma((3,)), dma((3,)),
            dma((3,)), dma((3,)),
            dma, dma,
            dma((TILES, QUADS)), dma((TILES, QUADS)),
            dma((TILES,)), dma((TILES,)),
            dma((TILES, QUADS)), dma((TILES, QUADS)),
            dma((TILES, 2, QUADS)), dma((TILES, 2, QUADS)),
            dma((9,)),
        ],
        compiler_params=pltpu.CompilerParams(
            collective_id=0, has_side_effects=True, vmem_limit_bytes=56 * 1024 * 1024
        ),
        name="window_backward",
    )(query_states, key_states, value_states, observed, closing_projector)


def solution(mesh):
    placed = (
        P("mem", "tok", None),
        P("mem", "tok", None),
        P("mem", "tok", None),
        P("tok", None),
        P(("tok", "mem"), None),
    )
    return jax.shard_map(
        body,
        mesh=mesh,
        in_specs=placed,
        out_specs=(P("mem", "tok", None), P("mem", "tok", None), P("mem", "tok", None)),
        check_vma=False,
    )
```
